512 devices in a mesh: side: 2 (over y_hi), vocab: 128 (over y_lo, x, z), tok: 2 (over core).
Axes of the slice: x: 4, y: 8 (y_hi: 2, y_lo: 4; y = y_hi * 4 + y_lo), z: 8, core: 2. Of those that a mesh axis runs over, the one named last changes fastest.
Arguments:
- reward_hidden: bfloat16 [2, 320, 2048], P('side', None, 'tok'), may hold values from -66 to 66
- reward_heads: bfloat16 [2, 2048, 151936], P('side', 'tok', 'vocab'), may hold values from -6 to 6
- policy_hidden: bfloat16 [320, 2048], P(None, ('side', 'tok')), may hold values from -66 to 66
- policy_head: bfloat16 [2048, 151936], P(('side', 'tok'), 'vocab'), may hold values from -6 to 6
- targets: int32 [320], replicated, may hold values from 0 to 151935
- response_mask: int32 [320], replicated, may hold values 0 or 1
- rollout_ids: int32 [320], replicated, may hold values from 0 to 3, never falling along the last dimension, each value on 1 to 160 neighbouring positions
Outputs:
- rewards: float32 [320], replicated
- hidden_grad: bfloat16 [320, 2048], P(None, ('side', 'tok'))
The draws below stay inside these ranges and needn't reach their ends.
All inputs are finite; a program needn't handle non-finite values.
Results may differ from the reference program's by a relative error of at most 0.005.
Values may be sent and summed in bfloat16 or wider, within the bound.
A program may use at most 64 MiB of HBM per device.

```python
import math
import jax
import jax.numpy as jnp
import numpy as np
from jax import lax

D = 2048
V = 151936
W = 320
ROLLOUTS = 4


def shared_parts(key, shape):
    key_base, key_unit = jax.random.split(key)
    base = jax.random.truncated_normal(key_base, -6.0, 6.0, shape, jnp.float32)
    unit = jax.random.uniform(key_unit, (shape[0], shape[1], 1), jnp.float32)
    return (base, unit)


def spread(unit, low, high):
    return jnp.exp(math.log(low) + unit * (math.log(high) - math.log(low)))


def hidden_rows(key, shape, low, high):
    base, unit = shared_parts(key, shape)
    return spread(unit, low, high) * base


def head_columns(key, shape_head, column_low, column_high):
    key = jax.random.fold_in(key, 5)
    key_weight, key_scale = jax.random.split(key, 2)
    column_scale = spread(jax.random.uniform(key_scale, (shape_head[0], 1, shape_head[2]), jnp.float32), column_low, column_high)
    heads = jax.random.truncated_normal(key_weight, -6.0, 6.0, shape_head, jnp.float32) * column_scale / math.sqrt(D)
    return heads


def draw_reward_hidden(key, part):
    values = hidden_rows(key, (2, W, D), 0.5, 2.5)
    return values.astype(jnp.bfloat16)


def draw_reward_heads(key, part):
    values = head_columns(key, (2, D, V), 0.6, 3.0)
    return values.astype(jnp.bfloat16)


def draw_policy_hidden(key, part):
    key = jax.random.fold_in(key, 7)
    values = hidden_rows(key, (1, W, D), 0.5, 2.5)
    return values[0].astype(jnp.bfloat16)


def draw_policy_head(key, part):
    key = jax.random.fold_in(key, 7)
    values = head_columns(key, (1, D, V), 0.6, 3.0)
    return values[0].astype(jnp.bfloat16)


def plant(result, own_key, least, largest):
    spot = [jax.random.randint(jax.random.fold_in(own_key, axis), (), 0, length) for axis, length in enumerate(result.shape)]
    longest = result.shape.index(max(result.shape))
    neighbour = spot[:longest] + [(spot[longest] + 1) % result.shape[longest]] + spot[longest + 1:]
    return result.at[tuple(spot)].set(least).at[tuple(neighbour)].set(largest)


def profile(amount, total, reach, slope):
    portions = [(1 << 20) // math.isqrt(rank ** slope) + 1 for rank in range(2, amount + 1)]
    spare, counts = total - reach - (amount - 1), [1] * (amount - 1)
    while spare > 0:
        candidates = [i for i in range(amount - 1) if counts[i] < reach]
        whole, remaining = sum([portions[i] for i in candidates]), spare
        for i in candidates:
            extra = min(reach - counts[i], max(1, remaining * portions[i] // whole), spare)
            counts[i] = counts[i] + extra
            spare = spare - extra
    return np.array([reach] + counts)


def uneven(stream_key, number_of, total, reach, slope):
    if number_of == 2:
        one = jax.random.randint(stream_key, (), max(1, total - reach), min(reach, total - 1) + 1)
        return jnp.stack([one, total - one])
    lengths = jnp.asarray(profile(number_of, total, reach, slope), jnp.int32)
    couples = (number_of - 1) // 2
    source_of, sink = lengths[1:1 + 2 * couples:2], lengths[2:2 + 2 * couples:2]
    margin = jnp.minimum(source_of - 1, reach - sink)
    shifted = jax.random.randint(jax.random.fold_in(stream_key, 1), (couples,), 0, 1 << 20) % (margin + 1)
    lengths = lengths.at[1:1 + 2 * couples:2].set(source_of - shifted).at[2:2 + 2 * couples:2].set(sink + shifted)
    return lengths[jax.random.permutation(jax.random.fold_in(stream_key, 2), number_of)]


def setup_inputs(seed: int = 0) -> dict:
    arg_keys = jax.random.split(jax.random.key(seed), 8)
    return {
        "reward_hidden": draw_reward_hidden(jax.random.fold_in(arg_keys[7], 71), 0),
        "reward_heads": draw_reward_heads(jax.random.fold_in(arg_keys[7], 71), 0),
        "policy_hidden": draw_policy_hidden(jax.random.fold_in(arg_keys[7], 71), 0),
        "policy_head": draw_policy_head(jax.random.fold_in(arg_keys[7], 71), 0),
        "targets": plant(jax.random.randint(arg_keys[4], (W,), 0, V), jax.random.fold_in(arg_keys[4], 1), 0, V - 1).astype(jnp.int32),
        "response_mask": plant((jax.random.randint(arg_keys[5], (W,), 0, 4) < 3).astype(jnp.int32), jax.random.fold_in(arg_keys[5], 1), 0, 1),
        "rollout_ids": jnp.searchsorted(jnp.cumsum(uneven(arg_keys[6], ROLLOUTS, W, W // 2, 0)), jnp.arange(W), side="right").astype(jnp.int32),
    }


BETA = 0.05


def reference(reward_hidden, reward_heads, policy_hidden, policy_head, targets, response_mask, rollout_ids):
    logprob_list = []
    for side_index in range(2):
        logits = jnp.dot(reward_hidden[side_index], reward_heads[side_index], preferred_element_type=jnp.float32)
        totals = jax.nn.logsumexp(logits, axis=1)
        picked = jnp.take_along_axis(logits, targets[:, None].astype(jnp.int32), axis=1)[:, 0]
        logprob_list.append(picked - totals)
    live_tokens = response_mask.astype(jnp.float32)
    rewards = BETA * live_tokens * (logprob_list[0] - logprob_list[1])
    row_index = jnp.arange(W, dtype=jnp.int32)
    same_rollout = (rollout_ids[:, None] == rollout_ids[None, :]) & (row_index[None, :] >= row_index[:, None])
    returns = jnp.sum(jnp.where(same_rollout, rewards[None, :], jnp.float32(0.0)), axis=1)
    token_weight = live_tokens * returns
    policy_logits = jnp.dot(policy_hidden, policy_head, preferred_element_type=jnp.float32)
    policy_probs = jax.nn.softmax(policy_logits, axis=1)
    columns = jnp.arange(V, dtype=jnp.int32)
    onehot = (columns[None, :] == targets[:, None]).astype(jnp.float32)
    logit_grad = (token_weight[:, None] * (policy_probs - onehot)).astype(jnp.bfloat16)
    hidden_grad = lax.dot_general(logit_grad, policy_head, (((1,), (1,)), ((), ())), preferred_element_type=jnp.float32)
    return rewards, hidden_grad.astype(jnp.bfloat16)
```

```python
import functools
import math

import jax
import jax.numpy as jnp
from jax import lax
from jax.experimental import pallas as pl
from jax.experimental.pallas import tpu as pltpu
from jax.sharding import PartitionSpec as P

BETA = 0.05
MESH = pl.DeviceIdType.MESH
F32 = jnp.float32
NX, NYL, NZ = 4, 4, 8
NY = 2 * NYL
W = 320
HALF = 160
RC = 32
NCH = HALF // RC
CR = 2 * RC
ZR = CR // NZ
LANES = 128
STEP = math.log(2.0) / 16.0
FULL = 32700.0
LOW = -1e30
NSEM = 256


def nt_dot(a, b):
    return lax.dot_general(a, b, (((1,), (1,)), ((), ())), preferred_element_type=F32)


def kernel(
    v,
    rh_hbm, rw_hbm, ph_hbm, pw_hbm, colinfo, rowinfo,
    rew, hg,
    rh, rw, ph, pw, pp, pr, qs, qr, eb, st,
    rp, rr, gs, xr, zs, zr, yr, zag, hx,
    hs, hxr, hz, hzr, hfin, rz, rx, ry, rc, wv,
    load_sem, send_sem, recv_sem,
):
    vp = pp.shape[1]
    feats = ph.shape[1]
    side = lax.axis_index("side")
    vocab = lax.axis_index("vocab")
    tok = lax.axis_index("tok")
    ylo = lax.div(vocab, NX * NZ)
    x = lax.rem(lax.div(vocab, NZ), NX)
    z = lax.rem(vocab, NZ)
    y = side * NYL + ylo
    first = vocab * v

    def at(yy, xx, zz, tt):
        return (lax.div(yy, NYL), lax.rem(yy, NYL) * (NX * NZ) + xx * NZ + zz, tt)

    core_peer = at(y, x, z, 1 - tok)
    side_peer = at(lax.rem(y + NYL, NY), x, z, tok)
    xs = [lax.rem(x + d, NX) for d in range(NX)]
    zs_ = [lax.rem(z + d, NZ) for d in range(NZ)]
    x_peer = [at(y, xs[d], z, tok) for d in range(NX)]
    z_peer = [at(y, x, zs_[d], tok) for d in range(NZ)]
    y_peer = [at(lax.rem(y + d, NY), x, z, tok) for d in range(NY)]
    yls = [lax.rem(ylo + d, NYL) for d in range(NYL)]
    yl_peer = [at(side * NYL + yls[d], x, z, tok) for d in range(NYL)]

    loads = [
        pltpu.make_async_copy(ph_hbm, ph, load_sem.at[0]),
        pltpu.make_async_copy(pw_hbm, pw, load_sem.at[1]),
        pltpu.make_async_copy(rh_hbm.at[0], rh, load_sem.at[2]),
        pltpu.make_async_copy(rw_hbm.at[0], rw, load_sem.at[3]),
    ]
    for c in loads:
        c.start()

    barrier = pltpu.get_barrier_semaphore()
    peers = [core_peer] + x_peer[1:] + z_peer[1:] + y_peer[1:]
    for p in peers:
        pl.semaphore_signal(barrier, inc=1, device_id=p, device_id_type=MESH)

    copies = []

    def send(src, dst, peer):
        i = len(copies)
        c = pltpu.make_async_remote_copy(
            src_ref=src, dst_ref=dst, send_sem=send_sem.at[i], recv_sem=recv_sem.at[i],
            device_id=peer, device_id_type=MESH,
        )
        c.start()
        copies.append(c)
        return c

    def landed(group):
        for c in group:
            c.wait_recv()

    tail = vp - LANES
    for buf in (pp, rp):
        buf[:, tail:] = jnp.zeros((W, LANES), F32)
    eb[:, tail:] = jnp.zeros((W, LANES), eb.dtype)

    own = pl.multiple_of(tok * HALF, HALF)
    other = pl.multiple_of((1 - tok) * HALF, HALF)

    loads[0].wait()
    loads[1].wait()
    pp[pl.ds(other, HALF), :v] = jnp.dot(ph[pl.ds(other, HALF), :], pw[...], preferred_element_type=F32)
    pl.semaphore_wait(barrier, len(peers))
    core_p = []
    for c in range(NCH):
        core_p.append(send(pp.at[pl.ds(other + RC * c, RC), :], pr.at[pl.ds(RC * c, RC), :], core_peer))
    pp[pl.ds(own, HALF), :v] = jnp.dot(ph[pl.ds(own, HALF), :], pw[...], preferred_element_type=F32)

    lane = lax.broadcasted_iota(jnp.int32, (RC, vp), 1)
    st_lane = lax.broadcasted_iota(jnp.int32, (RC, LANES), 1)

    side_p = []
    for c in range(NCH):
        landed([core_p[c]])
        rows = pl.ds(pl.multiple_of(own + RC * c, RC), RC)
        part = pp[rows, :] + pr[pl.ds(RC * c, RC), :]
        pp[rows, :] = part
        top = jnp.maximum(jnp.max(jnp.abs(part), axis=1, keepdims=True), 1e-6)
        expo = jnp.ceil(jnp.log(top) / STEP)
        inv = FULL * jnp.exp(expo * -STEP)
        quant = jnp.clip(jnp.round(part * inv), -32767.0, 32767.0)
        quant = jnp.where(lane == vp - 1, expo, quant)
        qs[pl.ds(RC * c, RC), :] = quant.astype(jnp.int32).astype(jnp.int16)
        side_p.append(send(qs.at[pl.ds(RC * c, RC), :], qr.at[pl.ds(RC * c, RC), :], side_peer))

    wide = lax.broadcasted_iota(jnp.int32, (W, v), 1) + first
    hot = (wide == colinfo[:, 0:1]).astype(jnp.bfloat16)
    picked = nt_dot(hot, pw[...]).astype(jnp.bfloat16)
    for i in range(NX):
        hs[i] = picked[:, LANES * i:LANES * (i + 1)]
    h_x = [send(hs.at[xs[d]], hxr.at[d - 1], x_peer[d]) for d in range(1, NX)]

    loads[2].wait()
    loads[3].wait()
    rp[pl.ds(other, HALF), :v] = jnp.dot(rh[pl.ds(other, HALF), :], rw[...], preferred_element_type=F32)
    core_r = send(rp.at[pl.ds(other, HALF), :], rr, core_peer)
    rp[pl.ds(own, HALF), :v] = jnp.dot(rh[pl.ds(own, HALF), :], rw[...], preferred_element_type=F32)
    landed([core_r])
    stats = []
    for c in range(NCH):
        rows = pl.ds(pl.multiple_of(own + RC * c, RC), RC)
        logit = rp[rows, :] + rr[pl.ds(RC * c, RC), :]
        logit = jnp.where(lane < v, logit, LOW)
        m = jnp.max(logit, axis=1, keepdims=True)
        s = jnp.sum(jnp.exp(logit - m), axis=1, keepdims=True)
        is_target = (lane + first == colinfo[rows, 0:1]) & (lane < v)
        pick = jnp.sum(jnp.where(is_target, logit, 0.0), axis=1, keepdims=True)
        stats.append(jnp.where(st_lane == 0, m, jnp.where(st_lane == 1, s, jnp.where(st_lane == 2, pick, 0.0))))
    stats.append(jnp.zeros((256 - HALF, LANES), F32))
    rz[z] = jnp.transpose(jnp.concatenate(stats, axis=0))[:8, :]
    r_z = [send(rz.at[z], rz.at[z], z_peer[d]) for d in range(1, NZ)]

    def merge_rows(buf, lo, hi):
        tiles = [buf[i] for i in range(lo, hi)]
        m = tiles[0][0:1]
        for t in tiles[1:]:
            m = jnp.maximum(m, t[0:1])
        s = jnp.zeros_like(m)
        pick = jnp.zeros_like(m)
        for t in tiles:
            s = s + jnp.exp(t[0:1] - m) * t[1:2]
            pick = pick + t[2:3]
        return m, s, pick

    def pack_rows(m, s, pick):
        row = lax.broadcasted_iota(jnp.int32, (8, 256), 0)
        return jnp.where(row == 0, m, jnp.where(row == 1, s, jnp.where(row == 2, pick, 0.0)))

    landed(h_x)
    h_own = hs[x].astype(F32)
    for d in range(1, NX):
        h_own = h_own + hxr[d - 1].astype(F32)
    hz[...] = h_own.reshape(2, NCH, RC, LANES)
    per_blk = RC // ZR

    def z_part(ref, zz):
        return ref.at[lax.div(zz, per_blk), :, pl.ds(pl.multiple_of(lax.rem(zz, per_blk) * ZR, ZR), ZR), :]

    h_z = [send(z_part(hz, zs_[d]), hzr.at[d - 1], z_peer[d]) for d in range(1, NZ)]

    def r2():
        landed(r_z)
        rx[x] = pack_rows(*merge_rows(rz, 0, NZ))
        return [send(rx.at[x], rx.at[x], x_peer[d]) for d in range(1, NX)]

    def r3(r_x):
        landed(r_x)
        ry[y] = pack_rows(*merge_rows(rx, 0, NX))
        return [send(ry.at[y], ry.at[y], y_peer[d]) for d in range(1, NY)]

    def r4(r_y):
        landed(r_y)
        logp = []
        for s_ in range(2):
            m, s, pick = merge_rows(ry, s_ * NYL, (s_ + 1) * NYL)
            logp.append(pick - m - jnp.log(s))
        live = rowinfo[0:1, pl.ds(pl.multiple_of(tok * 256, 256), 256)].astype(F32)
        rc[tok] = jnp.broadcast_to(BETA * live * (logp[0] - logp[1]), (8, 256))
        return [send(rc.at[tok], rc.at[tok], core_peer)]

    def first_token(c):
        return pl.multiple_of(lax.div(z, per_blk) * HALF + RC * c + lax.rem(z, per_blk) * ZR, ZR)

    def r5(r_c):
        landed(r_c)
        row = jnp.concatenate([rc[0], rc[1]], axis=1)
        rew[...] = row
        spot = lax.broadcasted_iota(jnp.int32, (ZR, 512), 1)
        block = spot // 256
        inside = spot - 256 * block
        token = block * HALF + inside
        for c in range(NCH):
            t0 = first_token(c)
            mine = t0 + lax.broadcasted_iota(jnp.int32, (ZR, 512), 0)
            info = colinfo[pl.ds(t0, ZR), :]
            same = (info[:, 2:3] == rowinfo[1:2, :]) & (token >= mine) & (inside < HALF)
            ret = jnp.sum(jnp.where(same, row[:ZR], 0.0), axis=1, keepdims=True)
            wv[c] = jnp.broadcast_to(ret * info[:, 1:2].astype(F32), (ZR, LANES))

    def h3():
        landed(h_z)
        total = z_part(hz, z)[...]
        for d in range(1, NZ):
            total = total + hzr[d - 1]
        hfin[...] = total

    live_copies = {}

    def stage_a(c):
        landed([side_p[c]])
        rows = pl.ds(pl.multiple_of(own + RC * c, RC), RC)
        q = qr[pl.ds(RC * c, RC), :].astype(jnp.int32).astype(F32)
        scale = jnp.exp(q[:, vp - 1:vp] * STEP) * (1.0 / FULL)
        logit = jnp.where(lane < v, pp[rows, :] + q * scale, LOW)
        m = jnp.max(logit, axis=1, keepdims=True)
        e = jnp.exp(logit - m)
        is_target = (lane + first == colinfo[rows, 0:1]) & (lane < v)
        e_rest = jnp.where(is_target, 0.0, e)
        s_rest = jnp.sum(e_rest, axis=1, keepdims=True)
        s_target = jnp.sum(jnp.where(is_target, e, 0.0), axis=1, keepdims=True)
        eb[rows, :] = e_rest.astype(eb.dtype)
        st[rows, :] = jnp.where(st_lane == 0, m, jnp.where(st_lane == 1, s_rest, s_target))
        live_copies["e", c] = [
            send(eb.at[rows, :], eb.at[rows, :], core_peer),
            send(st.at[rows, :], st.at[rows, :], core_peer),
        ]

    def stage_b(c):
        landed(live_copies["e", c])
        r0, r1 = RC * c, HALF + RC * c
        e = jnp.concatenate([eb[r0:r0 + RC, :v], eb[r1:r1 + RC, :v]], axis=0)
        s = jnp.concatenate([st[r0:r0 + RC, :], st[r1:r1 + RC, :]], axis=0)
        g = nt_dot(e, pw[...])
        for i in range(NX):
            gs[c, i, 0] = g[:, LANES * i:LANES * (i + 1)]
            gs[c, i, 1] = s
        live_copies["x", c] = [send(gs.at[c, xs[d]], xr.at[c, d - 1], x_peer[d]) for d in range(1, NX)]

    def merge(gl, sl):
        m = sl[0][:, 0:1]
        for s in sl[1:]:
            m = jnp.maximum(m, s[:, 0:1])
        g_all = s_all = None
        for g, s in zip(gl, sl):
            a = jnp.exp(s[:, 0:1] - m)
            g_all = a * g if g_all is None else g_all + a * g
            s_all = a * s if s_all is None else s_all + a * s
        ln = lax.broadcasted_iota(jnp.int32, s_all.shape, 1)
        return g_all, jnp.where(ln == 0, m, s_all)

    def stage_c(c):
        landed(live_copies["x", c])
        gl = [gs[c, x, 0]] + [xr[c, d, 0] for d in range(NX - 1)]
        sl = [gs[c, x, 1]] + [xr[c, d, 1] for d in range(NX - 1)]
        g, s = merge(gl, sl)
        zs[c, 0] = g
        zs[c, 1] = s
        live_copies["z", c] = [
            send(zs.at[c, :, pl.ds(pl.multiple_of(zs_[d] * ZR, ZR), ZR), :], zr.at[c, d - 1], z_peer[d])
            for d in range(1, NZ)
        ]

    def stage_d(c):
        landed(live_copies["z", c])
        mine = pl.ds(pl.multiple_of(z * ZR, ZR), ZR)
        gl = [zs[c, 0, mine, :]] + [zr[c, d, 0] for d in range(NZ - 1)]
        sl = [zs[c, 1, mine, :]] + [zr[c, d, 1] for d in range(NZ - 1)]
        g, s = merge(gl, sl)
        yr[c, ylo, 0] = g
        yr[c, ylo, 1] = s
        yr[c, ylo, 2] = hfin[c]
        live_copies["y", c] = [send(yr.at[c, ylo], yr.at[c, ylo], yl_peer[d]) for d in range(1, NYL)]

    def stage_e(c):
        landed(live_copies["y", c])
        g, s = merge([yr[c, i, 0] for i in range(NYL)], [yr[c, i, 1] for i in range(NYL)])
        h = yr[c, 0, 2]
        for i in range(1, NYL):
            h = h + yr[c, i, 2]
        rest, target = s[:, 1:2], s[:, 2:3]
        scale = wv[c] / (rest + target)
        mine = pl.ds(pl.multiple_of(z * ZR, ZR), ZR)
        zag[c, mine, :] = scale * (g - rest * h)
        live_copies["zag", c] = [send(zag.at[c, mine, :], zag.at[c, mine, :], z_peer[d]) for d in range(1, NZ)]

    def stage_f(c):
        landed(live_copies["zag", c])
        hx[c, x] = zag[c].astype(hx.dtype)
        live_copies["xag", c] = [send(hx.at[c, x], hx.at[c, x], x_peer[d]) for d in range(1, NX)]

    def stage_g(c):
        landed(live_copies["xag", c])
        for i in range(NX):
            for b in range(2):
                hg[HALF * b + RC * c:HALF * b + RC * (c + 1), LANES * i:LANES * (i + 1)] = hx[c, i, RC * b:RC * (b + 1), :]

    r_x = r2()
    r_y = r_c = None
    stages = [stage_c, stage_d, stage_e, stage_f, stage_g]
    for k in range(NCH + 5):
        if k < NCH:
            stage_a(k)
        if k == 1:
            r_y = r3(r_x)
        if k == 2:
            r_c = r4(r_y)
            h3()
        if k == 3:
            r5(r_c)
        for j in range(2):
            if 0 <= k - 1 - j < NCH:
                stages[j](k - 1 - j)
            if j == 0 and k < NCH:
                stage_b(k)
        for j in range(2, 5):
            if 0 <= k - 1 - j < NCH:
                stages[j](k - 1 - j)
    for c in copies:
        c.wait_send()


def per_device(rh, rw, ph, pw, targets, mask, ids):
    v = rw.shape[2]
    feats, depth = ph.shape[1], rh.shape[2]
    vp = -(-v // LANES) * LANES
    if vp == v:
        vp += LANES
    info = jnp.stack([targets, mask, ids], axis=1)
    colinfo = jnp.pad(info, ((0, 0), (0, LANES - 3)))
    rowinfo = jnp.pad(jnp.stack([mask, ids]).reshape(2, 2, HALF), ((0, 6), (0, 0), (0, 256 - HALF)))
    rowinfo = rowinfo.reshape(8, 512)
    bf, i16 = jnp.bfloat16, jnp.int16
    vm = pltpu.VMEM
    scratch = [
        vm((W, depth), bf), vm((depth, v), bf), vm((W, feats), bf), vm((feats, v), bf),
        vm((W, vp), F32), vm((HALF, vp), F32), vm((HALF, vp), i16), vm((HALF, vp), i16),
        vm((W, vp), bf), vm((W, LANES), F32),
        vm((W, vp), F32), vm((HALF, vp), F32),
        vm((NCH, NX, 2, CR, LANES), F32), vm((NCH, NX - 1, 2, CR, LANES), F32),
        vm((NCH, 2, CR, LANES), F32), vm((NCH, NZ - 1, 2, ZR, LANES), F32),
        vm((NCH, NYL, 3, ZR, LANES), F32), vm((NCH, CR, LANES), F32), vm((NCH, NX, CR, LANES), bf),
        vm((NX, W, LANES), bf), vm((NX - 1, W, LANES), bf), vm((2, NCH, RC, LANES), F32),
        vm((NZ - 1, NCH, ZR, LANES), F32), vm((NCH, ZR, LANES), F32),
        vm((NZ, 8, 256), F32), vm((NX, 8, 256), F32), vm((NY, 8, 256), F32), vm((2, 8, 256), F32),
        vm((NCH, ZR, LANES), F32),
        pltpu.SemaphoreType.DMA((4,)), pltpu.SemaphoreType.DMA((NSEM,)), pltpu.SemaphoreType.DMA((NSEM,)),
    ]
    anyspec = pl.BlockSpec(memory_space=pl.ANY)
    vspec = pl.BlockSpec(memory_space=pltpu.VMEM)
    rew, hg = pl.pallas_call(
        functools.partial(kernel, v),
        out_shape=(jax.ShapeDtypeStruct((8, 512), F32), jax.ShapeDtypeStruct((W, feats), bf)),
        in_specs=[anyspec] * 4 + [vspec] * 2,
        out_specs=(vspec, vspec),
        scratch_shapes=scratch,
        compiler_params=pltpu.CompilerParams(
            collective_id=0, has_side_effects=True, vmem_limit_bytes=56 << 20
        ),
    )(rh, rw, ph, pw, colinfo, rowinfo)
    rewards = jnp.concatenate([rew[0, :HALF], rew[0, 256:256 + HALF]])
    return rewards, hg


def solution(mesh):
    placed = (
        P("side", None, "tok"),
        P("side", "tok", "vocab"),
        P(None, ("side", "tok")),
        P(("side", "tok"), "vocab"),
        P(),
        P(),
        P(),
    )
    return jax.shard_map(
        per_device,
        mesh=mesh,
        in_specs=placed,
        out_specs=(P(), P(None, ("side", "tok"))),
        check_vma=False,
    )
```

```python
import functools
import math

import jax
import jax.numpy as jnp
from jax import lax
from jax.experimental import pallas as pl
from jax.experimental.pallas import tpu as pltpu
from jax.sharding import PartitionSpec as P

BETA = 0.05
MESH = pl.DeviceIdType.MESH
F32 = jnp.float32
NX, NYL, NZ = 4, 4, 8
NY = 2 * NYL
W = 320
HALF = 160
RC = 32
NCH = HALF // RC
SR = 16
WINDOW = 4
CR = 2 * RC
ZR = CR // NZ
LANES = 128
STEP = math.log(2.0) / 16.0
FULL = 32700.0
LOW = -1e30
NSEM = 256


def nt_dot(a, b):
    return lax.dot_general(a, b, (((1,), (1,)), ((), ())), preferred_element_type=F32)


def kernel(
    v,
    rh_hbm, rw_hbm, ph_hbm, pw_hbm, t_hbm, m_hbm, i_hbm,
    rew, hg,
    rh, rw, ph, pw, pp, pr, qs, qr, eb, st,
    rp, rr, gs, xr, zs, zr, yr, zag, hx,
    hs, hxr, hz, hzr, hfin, rz, rx, ry, rc, wv, colinfo, rowinfo, targets, mask, ids,
    load_sem, send_sem, recv_sem,
):
    vp = pp.shape[1]
    feats = ph.shape[1]
    side = lax.axis_index("side")
    vocab = lax.axis_index("vocab")
    tok = lax.axis_index("tok")
    ylo = lax.div(vocab, NX * NZ)
    x = lax.rem(lax.div(vocab, NZ), NX)
    z = lax.rem(vocab, NZ)
    y = side * NYL + ylo
    first = vocab * v

    def at(yy, xx, zz, tt):
        return (lax.div(yy, NYL), lax.rem(yy, NYL) * (NX * NZ) + xx * NZ + zz, tt)

    core_peer = at(y, x, z, 1 - tok)
    side_peer = at(lax.rem(y + NYL, NY), x, z, tok)
    xs = [lax.rem(x + d, NX) for d in range(NX)]
    zs_ = [lax.rem(z + d, NZ) for d in range(NZ)]
    x_peer = [at(y, xs[d], z, tok) for d in range(NX)]
    z_peer = [at(y, x, zs_[d], tok) for d in range(NZ)]
    y_peer = [at(lax.rem(y + d, NY), x, z, tok) for d in range(NY)]
    yls = [lax.rem(ylo + d, NYL) for d in range(NYL)]
    yl_peer = [at(side * NYL + yls[d], x, z, tok) for d in range(NYL)]

    loads = []

    def load(src, dst, pieces=1):
        step = -(-src.shape[0] // (16 * pieces)) * 16
        group = []
        for r in range(0, src.shape[0], step):
            part = pl.ds(r, min(step, src.shape[0] - r))
            group.append(pltpu.make_async_copy(src.at[part], dst.at[part], load_sem.at[len(loads)]))
            loads.append(group[-1])
            group[-1].start()
        return group

    def loaded(group):
        for c in group:
            c.wait()

    policy = load(pw_hbm, pw, 4) + load(ph_hbm, ph)
    lists_in = [load(t_hbm, targets), load(m_hbm, mask), load(i_hbm, ids)]

    barrier = pltpu.get_barrier_semaphore()
    peers = [core_peer] + x_peer[1:] + z_peer[1:] + y_peer[1:]
    for p in peers:
        pl.semaphore_signal(barrier, inc=1, device_id=p, device_id_type=MESH)

    copies = []

    def send(src, dst, peer):
        i = len(copies)
        c = pltpu.make_async_remote_copy(
            src_ref=src, dst_ref=dst, send_sem=send_sem.at[i], recv_sem=recv_sem.at[i],
            device_id=peer, device_id_type=MESH,
        )
        c.start()
        copies.append(c)
        return c

    def landed(group):
        for c in group:
            c.wait_recv()

    for c in lists_in:
        loaded(c)
    lists = [r[...].reshape(1, W) for r in (targets, mask, ids)]
    rows3 = jnp.concatenate(lists + [jnp.zeros((5, W), jnp.int32)], axis=0).astype(F32)
    rows3 = jnp.concatenate([rows3, jnp.zeros((LANES - 8, W), F32)], axis=0)
    rows3 = jnp.concatenate([rows3, jnp.zeros((LANES, 384 - W), F32)], axis=1)
    colinfo[...] = jnp.transpose(rows3)[:W].astype(jnp.int32)
    for b in range(2):
        half = jnp.concatenate([r[:, HALF * b:HALF * (b + 1)] for r in lists[1:]], axis=0)
        rowinfo[0:2, 256 * b:256 * b + HALF] = half
        rowinfo[0:2, 256 * b + HALF:256 * (b + 1)] = jnp.zeros((2, 256 - HALF), jnp.int32)

    tail = vp - LANES
    for buf in (pp, rp):
        buf[:, tail:] = jnp.zeros((W, LANES), F32)
    eb[:, tail:] = jnp.zeros((W, LANES), eb.dtype)

    own = pl.multiple_of(tok * HALF, HALF)
    other = pl.multiple_of((1 - tok) * HALF, HALF)

    loaded(policy)
    reward = load(rh_hbm.at[0], rh) + load(rw_hbm.at[0], rw, 4)
    pp[pl.ds(other, HALF), :v] = nt_dot(ph[pl.ds(other, HALF), :], pw[...])
    pl.semaphore_wait(barrier, len(peers))
    core_p = []
    for c in range(NCH):
        core_p.append(send(pp.at[pl.ds(other + RC * c, RC), :], pr.at[pl.ds(RC * c, RC), :], core_peer))
    pp[pl.ds(own, HALF), :v] = nt_dot(ph[pl.ds(own, HALF), :], pw[...])

    lane = lax.broadcasted_iota(jnp.int32, (RC, vp), 1)
    st_lane = lax.broadcasted_iota(jnp.int32, (RC, LANES), 1)

    side_p = []

    def side_send():
        rows = pl.ds(SR * len(side_p), SR)
        side_p.append(send(qs.at[rows, :], qr.at[rows, :], side_peer))

    def side_step(i):
        landed([side_p[i]])
        if len(side_p) < HALF // SR:
            side_p[i].wait_send()
            waited.append(side_p[i])
            side_send()

    waited = []
    for c in range(NCH):
        landed([core_p[c]])
        rows = pl.ds(pl.multiple_of(own + RC * c, RC), RC)
        part = pp[rows, :] + pr[pl.ds(RC * c, RC), :]
        pp[rows, :] = part
        top = jnp.maximum(jnp.max(jnp.abs(part), axis=1, keepdims=True), 1e-6)
        expo = jnp.ceil(jnp.log(top) / STEP)
        inv = FULL * jnp.exp(expo * -STEP)
        quant = jnp.clip(jnp.round(part * inv), -32767.0, 32767.0)
        quant = jnp.where(lane == vp - 1, expo, quant)
        qs[pl.ds(RC * c, RC), :] = quant.astype(jnp.int32).astype(jnp.int16)
        for _ in range(2):
            if len(side_p) < WINDOW:
                side_send()

    wide = lax.broadcasted_iota(jnp.int32, (W, v), 1) + first
    hot = (wide == colinfo[:, 0:1]).astype(jnp.bfloat16)
    picked = jnp.dot(hot, pw[...], preferred_element_type=F32).astype(jnp.bfloat16)
    for i in range(NX):
        hs[i] = picked[:, LANES * i:LANES * (i + 1)]
    h_x = [send(hs.at[xs[d]], hxr.at[d - 1], x_peer[d]) for d in range(1, NX)]

    loaded(reward)
    rp[pl.ds(other, HALF), :v] = nt_dot(rh[pl.ds(other, HALF), :], rw[...])
    core_r = send(rp.at[pl.ds(other, HALF), :], rr, core_peer)
    rp[pl.ds(own, HALF), :v] = nt_dot(rh[pl.ds(own, HALF), :], rw[...])
    def r1():
        landed([core_r])
        stats = []
        for c in range(NCH):
            rows = pl.ds(pl.multiple_of(own + RC * c, RC), RC)
            logit = rp[rows, :] + rr[pl.ds(RC * c, RC), :]
            logit = jnp.where(lane < v, logit, LOW)
            m = jnp.max(logit, axis=1, keepdims=True)
            s = jnp.sum(jnp.exp(logit - m), axis=1, keepdims=True)
            is_target = (lane + first == colinfo[rows, 0:1]) & (lane < v)
            pick = jnp.sum(jnp.where(is_target, logit, 0.0), axis=1, keepdims=True)
            stats.append(jnp.where(st_lane == 0, m, jnp.where(st_lane == 1, s, jnp.where(st_lane == 2, pick, 0.0))))
        stats.append(jnp.zeros((256 - HALF, LANES), F32))
        rz[z] = jnp.transpose(jnp.concatenate(stats, axis=0))[:8, :]
        return [send(rz.at[z], rz.at[z], z_peer[d]) for d in range(1, NZ)]

    def merge_rows(buf, lo, hi):
        tiles = [buf[i] for i in range(lo, hi)]
        m = tiles[0][0:1]
        for t in tiles[1:]:
            m = jnp.maximum(m, t[0:1])
        s = jnp.zeros_like(m)
        pick = jnp.zeros_like(m)
        for t in tiles:
            s = s + jnp.exp(t[0:1] - m) * t[1:2]
            pick = pick + t[2:3]
        return m, s, pick

    def pack_rows(m, s, pick):
        row = lax.broadcasted_iota(jnp.int32, (8, 256), 0)
        return jnp.where(row == 0, m, jnp.where(row == 1, s, jnp.where(row == 2, pick, 0.0)))

    def h2():
        landed(h_x)
        h_own = hs[x].astype(F32)
        for d in range(1, NX):
            h_own = h_own + hxr[d - 1].astype(F32)
        hz[...] = h_own.reshape(2, NCH, RC, LANES)
        return [send(z_part(hz, zs_[d]), hzr.at[d - 1], z_peer[d]) for d in range(1, NZ)]

    per_blk = RC // ZR

    def z_part(ref, zz):
        return ref.at[lax.div(zz, per_blk), :, pl.ds(pl.multiple_of(lax.rem(zz, per_blk) * ZR, ZR), ZR), :]

    def r2(r_z):
        landed(r_z)
        rx[x] = pack_rows(*merge_rows(rz, 0, NZ))
        return [send(rx.at[x], rx.at[x], x_peer[d]) for d in range(1, NX)]

    def r3(r_x):
        landed(r_x)
        ry[y] = pack_rows(*merge_rows(rx, 0, NX))
        return [send(ry.at[y], ry.at[y], y_peer[d]) for d in range(1, NY)]

    def r4(r_y):
        landed(r_y)
        logp = []
        for s_ in range(2):
            m, s, pick = merge_rows(ry, s_ * NYL, (s_ + 1) * NYL)
            logp.append(pick - m - jnp.log(s))
        live = rowinfo[0:1, pl.ds(pl.multiple_of(tok * 256, 256), 256)].astype(F32)
        rc[tok] = jnp.broadcast_to(BETA * live * (logp[0] - logp[1]), (8, 256))
        return [send(rc.at[tok], rc.at[tok], core_peer)]

    def r5(r_c):
        landed(r_c)
        row = jnp.concatenate([rc[0], rc[1]], axis=1)
        rew[...] = jnp.concatenate([rc[0, 0:1, :HALF], rc[1, 0:1, :HALF]], axis=1).reshape(W)
        spot = lax.broadcasted_iota(jnp.int32, (RC, 512), 1)
        block = spot // 256
        inside = spot - 256 * block
        token = block * HALF + inside
        for t0 in range(0, W, RC):
            mine = t0 + lax.broadcasted_iota(jnp.int32, (RC, 512), 0)
            info = colinfo[t0:t0 + RC, :]
            same = (info[:, 2:3] == rowinfo[1:2, :]) & (token >= mine) & (inside < HALF)
            ret = jnp.sum(jnp.where(same, row[0:1], 0.0), axis=1, keepdims=True)
            wv[t0:t0 + RC, :] = jnp.broadcast_to(ret * info[:, 1:2].astype(F32), (RC, LANES))

    def h3(h_z):
        landed(h_z)
        total = z_part(hz, z)[...]
        for d in range(1, NZ):
            total = total + hzr[d - 1]
        hfin[...] = total

    live_copies = {}

    def stage_a(c):
        rows = pl.ds(pl.multiple_of(own + RC * c, RC), RC)
        q = qr[pl.ds(RC * c, RC), :].astype(jnp.int32).astype(F32)
        scale = jnp.exp(q[:, vp - 1:vp] * STEP) * (1.0 / FULL)
        logit = jnp.where(lane < v, pp[rows, :] + q * scale, LOW)
        m = jnp.max(logit, axis=1, keepdims=True)
        e = jnp.exp(logit - m)
        is_target = (lane + first == colinfo[rows, 0:1]) & (lane < v)
        e_rest = jnp.where(is_target, 0.0, e)
        s_rest = jnp.sum(e_rest, axis=1, keepdims=True)
        s_target = jnp.sum(jnp.where(is_target, e, 0.0), axis=1, keepdims=True)
        eb[rows, :] = e_rest.astype(eb.dtype)
        st[rows, :] = jnp.where(st_lane == 0, m, jnp.where(st_lane == 1, s_rest, s_target))
        live_copies["e", c] = [
            send(eb.at[rows, :], eb.at[rows, :], core_peer),
            send(st.at[rows, :], st.at[rows, :], core_peer),
        ]

    def split3(s, ref):
        ln = lax.broadcasted_iota(jnp.int32, s.shape, 1)
        left = jnp.where(ln < 3, s[:, 0:1], jnp.where(ln < 6, s[:, 1:2], s[:, 2:3]))
        part = lax.rem(ln, 3)
        for i in range(2):
            ref[...] = left.astype(ref.dtype)
            left = jnp.where(part > i, left - ref[...].astype(F32), left)
        ref[...] = left.astype(ref.dtype)

    def stage_b(c):
        landed(live_copies["e", c])
        r0, r1 = RC * c, HALF + RC * c
        e = jnp.concatenate([eb[r0:r0 + RC, :v], eb[r1:r1 + RC, :v]], axis=0)
        split3(jnp.concatenate([st[r0:r0 + RC, :], st[r1:r1 + RC, :]], axis=0), gs.at[c, 0, 1])
        s = gs[c, 0, 1]
        g = jnp.dot(e, pw[...], preferred_element_type=F32)
        for i in range(NX):
            gs[c, i, 0] = g[:, LANES * i:LANES * (i + 1)].astype(gs.dtype)
            if i:
                gs[c, i, 1] = s
        live_copies["x", c] = [send(gs.at[c, xs[d]], xr.at[c, d - 1], x_peer[d]) for d in range(1, NX)]

    def merge(gl, sl):
        m = sl[0][:, 0:1]
        for s in sl[1:]:
            m = jnp.maximum(m, s[:, 0:1])
        g_all = s_all = None
        for g, s in zip(gl, sl):
            a = jnp.exp(s[:, 0:1] - m)
            g_all = a * g if g_all is None else g_all + a * g
            s_all = a * s if s_all is None else s_all + a * s
        ln = lax.broadcasted_iota(jnp.int32, s_all.shape, 1)
        return g_all, jnp.where(ln == 0, m, s_all)

    def merge_parts(gl, tl):
        tl = [t.astype(F32) for t in tl]
        ml = [t[:, 0:1] + t[:, 1:2] + t[:, 2:3] for t in tl]
        m = ml[0]
        for other_m in ml[1:]:
            m = jnp.maximum(m, other_m)
        g_all = t_all = None
        for g, t, mi in zip(gl, tl, ml):
            a = jnp.exp(mi - m)
            g = a * g.astype(F32)
            t = a * t
            g_all = g if g_all is None else g_all + g
            t_all = t if t_all is None else t_all + t
        ln = lax.broadcasted_iota(jnp.int32, t_all.shape, 1)
        r, s = (t_all[:, i:i + 1] + t_all[:, i + 1:i + 2] + t_all[:, i + 2:i + 3] for i in (3, 6))
        return g_all, jnp.where(ln == 0, m, jnp.where(ln == 1, r, s))

    def stage_c(c):
        landed(live_copies["x", c])
        gl = [gs[c, x, 0]] + [xr[c, d, 0] for d in range(NX - 1)]
        tl = [gs[c, x, 1]] + [xr[c, d, 1] for d in range(NX - 1)]
        g, s = merge_parts(gl, tl)
        zs[c, 0] = g
        zs[c, 1] = s
        live_copies["z", c] = [
            send(zs.at[c, :, pl.ds(pl.multiple_of(zs_[d] * ZR, ZR), ZR), :], zr.at[c, d - 1], z_peer[d])
            for d in range(1, NZ)
        ]

    def stage_d(c):
        landed(live_copies["z", c])
        mine = pl.ds(pl.multiple_of(z * ZR, ZR), ZR)
        gl = [zs[c, 0, mine, :]] + [zr[c, d, 0] for d in range(NZ - 1)]
        sl = [zs[c, 1, mine, :]] + [zr[c, d, 1] for d in range(NZ - 1)]
        g, s = merge(gl, sl)
        yr[c, ylo, 0] = g
        yr[c, ylo, 1] = s
        yr[c, ylo, 2] = hfin[c]
        live_copies["y", c] = [send(yr.at[c, ylo], yr.at[c, ylo], yl_peer[d]) for d in range(1, NYL)]

    def stage_e(c):
        landed(live_copies["y", c])
        g, s = merge([yr[c, i, 0] for i in range(NYL)], [yr[c, i, 1] for i in range(NYL)])
        h = yr[c, 0, 2]
        for i in range(1, NYL):
            h = h + yr[c, i, 2]
        rest, target = s[:, 1:2], s[:, 2:3]
        scale = 1.0 / (rest + target)
        mine = pl.ds(pl.multiple_of(z * ZR, ZR), ZR)
        zag[c, mine, :] = scale * (g - rest * h)
        live_copies["zag", c] = [send(zag.at[c, mine, :], zag.at[c, mine, :], z_peer[d]) for d in range(1, NZ)]

    def stage_f(c):
        landed(live_copies["zag", c])
        weight = jnp.concatenate([wv[RC * c:RC * (c + 1), :], wv[HALF + RC * c:HALF + RC * (c + 1), :]], axis=0)
        hx[c, x] = (weight * zag[c]).astype(hx.dtype)
        live_copies["xag", c] = [send(hx.at[c, x], hx.at[c, x], x_peer[d]) for d in range(1, NX)]

    def stage_g(c):
        landed(live_copies["xag", c])
        for i in range(NX):
            for b in range(2):
                hg[HALF * b + RC * c:HALF * b + RC * (c + 1), LANES * i:LANES * (i + 1)] = hx[c, i, RC * b:RC * (b + 1), :]

    chain = {
        "S": side_step, "A": stage_a, "B": stage_b, "C": stage_c, "D": stage_d, "E": stage_e, "F": stage_f, "G": stage_g,
    }
    order = (
        "S0", "r1", "S1", "A0", "B0", "S2", "h2", "S3", "A1", "B1", "C0", "r2", "S4", "S5", "A2",
        "B2", "C1", "h3", "D0", "r3", "S6", "S7", "A3", "B3", "C2", "D1", "E0", "S8", "S9", "A4",
        "B4", "C3", "D2", "E1", "r4", "C4", "D3", "E2", "r5", "F0", "D4", "E3", "F1", "G0", "E4",
        "F2", "G1", "F3", "G2", "F4", "G3", "G4",
    )
    for word in order:
        if word == "h2":
            h_z = h2()
        elif word == "h3":
            h3(h_z)
        elif word == "r1":
            r_z = r1()
        elif word == "r2":
            r_x = r2(r_z)
        elif word == "r3":
            r_y = r3(r_x)
        elif word == "r4":
            r_c = r4(r_y)
        elif word == "r5":
            r5(r_c)
        else:
            chain[word[0]](int(word[1:]))
    for c in copies:
        if all(c is not w for w in waited):
            c.wait_send()


def hand_over(rew, hg, rew_out, hg_out):
    rew_out[...] = rew[...]
    hg_out[...] = hg[...]


def per_device(rh, rw, ph, pw, targets, mask, ids):
    v = rw.shape[2]
    rw, pw = jnp.swapaxes(rw, 1, 2), jnp.swapaxes(pw, 0, 1)
    feats, depth = ph.shape[1], rh.shape[2]
    vp = -(-v // LANES) * LANES
    if vp == v:
        vp += LANES
    bf, i16 = jnp.bfloat16, jnp.int16
    vm = pltpu.VMEM
    scratch = [
        vm((W, depth), bf), vm((v, depth), bf), vm((W, feats), bf), vm((v, feats), bf),
        vm((W, vp), F32), vm((HALF, vp), F32), vm((HALF, vp), i16), vm((HALF, vp), i16),
        vm((W, vp), bf), vm((W, LANES), F32),
        vm((W, vp), F32), vm((HALF, vp), F32),
        vm((NCH, NX, 2, CR, LANES), bf), vm((NCH, NX - 1, 2, CR, LANES), bf),
        vm((NCH, 2, CR, LANES), F32), vm((NCH, NZ - 1, 2, ZR, LANES), F32),
        vm((NCH, NYL, 3, ZR, LANES), F32), vm((NCH, CR, LANES), F32), vm((NCH, NX, CR, LANES), bf),
        vm((NX, W, LANES), bf), vm((NX - 1, W, LANES), bf), vm((2, NCH, RC, LANES), F32),
        vm((NZ - 1, NCH, ZR, LANES), F32), vm((NCH, ZR, LANES), F32),
        vm((NZ, 8, 256), F32), vm((NX, 8, 256), F32), vm((NY, 8, 256), F32), vm((2, 8, 256), F32),
        vm((W, LANES), F32), vm((W, LANES), jnp.int32), vm((8, 512), jnp.int32),
        vm((W,), jnp.int32), vm((W,), jnp.int32), vm((W,), jnp.int32),
        pltpu.SemaphoreType.DMA((16,)), pltpu.SemaphoreType.DMA((NSEM,)), pltpu.SemaphoreType.DMA((NSEM,)),
    ]
    vspec = pl.BlockSpec(memory_space=pltpu.VMEM)
    hspec = pl.BlockSpec(memory_space=pltpu.HBM)
    rew, hg = pl.pallas_call(
        functools.partial(kernel, v),
        out_shape=(jax.ShapeDtypeStruct((W,), F32), jax.ShapeDtypeStruct((W, feats), bf)),
        in_specs=[hspec] * 7,
        out_specs=(vspec, vspec),
        scratch_shapes=scratch,
        compiler_params=pltpu.CompilerParams(
            collective_id=0, has_side_effects=True, vmem_limit_bytes=60 << 20
        ),
    )(rh, rw, ph, pw, targets, mask, ids)
    return pl.pallas_call(
        hand_over,
        out_shape=(jax.ShapeDtypeStruct((W,), F32), jax.ShapeDtypeStruct((W, feats), bf)),
        in_specs=[vspec, vspec],
        out_specs=(vspec, vspec),
    )(rew, hg)


def solution(mesh):
    placed = (
        P("side", None, "tok"),
        P("side", "tok", "vocab"),
        P(None, ("side", "tok")),
        P(("side", "tok"), "vocab"),
        P(),
        P(),
        P(),
    )
    return jax.shard_map(
        per_device,
        mesh=mesh,
        in_specs=placed,
        out_specs=(P(), P(None, ("side", "tok"))),
        check_vma=False,
    )
```

```python
import functools
import math

import jax
import jax.numpy as jnp
from jax import lax
from jax.experimental import pallas as pl
from jax.experimental.pallas import tpu as pltpu
from jax.sharding import PartitionSpec as P

BETA = 0.05
MESH = pl.DeviceIdType.MESH
F32 = jnp.float32
NX, NYL, NZ = 4, 4, 8
NY = 2 * NYL
W = 320
HALF = 160
RC = 32
NCH = HALF // RC
SR = 16
WINDOW = 4
CR = 2 * RC
ZR = CR // NZ
LANES = 128
STEP = math.log(2.0) / 16.0
FULL = 32700.0
LOW = -1e30
NSEM = 256


def nt_dot(a, b):
    return lax.dot_general(a, b, (((1,), (1,)), ((), ())), preferred_element_type=F32)


def kernel(
    v,
    rh_hbm, rw_hbm, ph_hbm, pw_hbm, t_hbm, m_hbm, i_hbm,
    rew, hg,
    rh, rw, ph, pw, pp, pr, qs, qr, eb, st,
    rp, rr, gs, xr, zs, zr, yr, zag, hx,
    hs, hxr, hz, hzr, hfin, rz, rx, ry, rc, wv, colinfo, rowinfo, targets, mask, ids,
    load_sem, send_sem, recv_sem,
):
    vp = pp.shape[1]
    feats = ph.shape[1]
    side = lax.axis_index("side")
    vocab = lax.axis_index("vocab")
    tok = lax.axis_index("tok")
    ylo = lax.div(vocab, NX * NZ)
    x = lax.rem(lax.div(vocab, NZ), NX)
    z = lax.rem(vocab, NZ)
    y = side * NYL + ylo
    first = vocab * v

    def at(yy, xx, zz, tt):
        return (lax.div(yy, NYL), lax.rem(yy, NYL) * (NX * NZ) + xx * NZ + zz, tt)

    core_peer = at(y, x, z, 1 - tok)
    side_peer = at(lax.rem(y + NYL, NY), x, z, tok)
    xs = [lax.rem(x + d, NX) for d in range(NX)]
    zs_ = [lax.rem(z + d, NZ) for d in range(NZ)]
    x_peer = [at(y, xs[d], z, tok) for d in range(NX)]
    z_peer = [at(y, x, zs_[d], tok) for d in range(NZ)]
    y_peer = [at(lax.rem(y + d, NY), x, z, tok) for d in range(NY)]
    yls = [lax.rem(ylo + d, NYL) for d in range(NYL)]
    yl_peer = [at(side * NYL + yls[d], x, z, tok) for d in range(NYL)]

    loads = []

    def load(src, dst, pieces=1):
        step = -(-src.shape[0] // (16 * pieces)) * 16
        group = []
        for r in range(0, src.shape[0], step):
            part = pl.ds(r, min(step, src.shape[0] - r))
            group.append(pltpu.make_async_copy(src.at[part], dst.at[part], load_sem.at[len(loads)]))
            loads.append(group[-1])
            group[-1].start()
        return group

    def loaded(group):
        for c in group:
            c.wait()

    policy = load(pw_hbm, pw, 4) + load(ph_hbm, ph)
    lists_in = [load(t_hbm, targets), load(m_hbm, mask), load(i_hbm, ids)]

    barrier = pltpu.get_barrier_semaphore()
    peers = [core_peer] + x_peer[1:] + z_peer[1:] + y_peer[1:]
    for p in peers:
        pl.semaphore_signal(barrier, inc=1, device_id=p, device_id_type=MESH)

    copies = []

    def send(src, dst, peer):
        i = len(copies)
        c = pltpu.make_async_remote_copy(
            src_ref=src, dst_ref=dst, send_sem=send_sem.at[i], recv_sem=recv_sem.at[i],
            device_id=peer, device_id_type=MESH,
        )
        c.start()
        copies.append(c)
        return c

    def landed(group):
        for c in group:
            c.wait_recv()

    for c in lists_in:
        loaded(c)
    lists = [r[...].reshape(1, W) for r in (targets, mask, ids)]
    rows3 = jnp.concatenate(lists + [jnp.zeros((5, W), jnp.int32)], axis=0).astype(F32)
    rows3 = jnp.concatenate([rows3, jnp.zeros((LANES - 8, W), F32)], axis=0)
    rows3 = jnp.concatenate([rows3, jnp.zeros((LANES, 384 - W), F32)], axis=1)
    colinfo[...] = jnp.transpose(rows3)[:W].astype(jnp.int32)
    for b in range(2):
        half = jnp.concatenate([r[:, HALF * b:HALF * (b + 1)] for r in lists[1:]], axis=0)
        rowinfo[0:2, 256 * b:256 * b + HALF] = half
        rowinfo[0:2, 256 * b + HALF:256 * (b + 1)] = jnp.zeros((2, 256 - HALF), jnp.int32)

    tail = vp - LANES
    for buf in (pp, rp):
        buf[:, tail:] = jnp.zeros((W, LANES), F32)
    eb[:, tail:] = jnp.zeros((W, LANES), eb.dtype)

    own = pl.multiple_of(tok * HALF, HALF)
    other = pl.multiple_of((1 - tok) * HALF, HALF)

    loaded(policy)
    reward = load(rh_hbm.at[0], rh) + load(rw_hbm.at[0], rw, 4)
    pp[pl.ds(other, HALF), :v] = nt_dot(ph[pl.ds(other, HALF), :], pw[...])
    pl.semaphore_wait(barrier, len(peers))
    core_p = []
    for c in range(NCH):
        core_p.append(send(pp.at[pl.ds(other + RC * c, RC), :], pr.at[pl.ds(RC * c, RC), :], core_peer))
    pp[pl.ds(own, HALF), :v] = nt_dot(ph[pl.ds(own, HALF), :], pw[...])

    lane = lax.broadcasted_iota(jnp.int32, (RC, vp), 1)
    st_lane = lax.broadcasted_iota(jnp.int32, (RC, LANES), 1)

    side_p = []

    def side_send():
        rows = pl.ds(SR * len(side_p), SR)
        side_p.append(send(qs.at[rows, :], qr.at[rows, :], side_peer))

    def side_step(i):
        landed([side_p[i]])
        if len(side_p) < HALF // SR:
            side_p[i].wait_send()
            waited.append(side_p[i])
            side_send()

    waited = []
    for c in range(NCH):
        landed([core_p[c]])
        rows = pl.ds(pl.multiple_of(own + RC * c, RC), RC)
        part = pp[rows, :] + pr[pl.ds(RC * c, RC), :]
        pp[rows, :] = part
        top = jnp.maximum(jnp.max(jnp.abs(part), axis=1, keepdims=True), 1e-6)
        expo = jnp.ceil(jnp.log(top) / STEP)
        inv = FULL * jnp.exp(expo * -STEP)
        quant = jnp.clip(jnp.round(part * inv), -32767.0, 32767.0)
        quant = jnp.where(lane == vp - 1, expo, quant)
        qs[pl.ds(RC * c, RC), :] = quant.astype(jnp.int32).astype(jnp.int16)
        for _ in range(2):
            if len(side_p) < WINDOW:
                side_send()

    wide = lax.broadcasted_iota(jnp.int32, (W, v), 1) + first
    hot = (wide == colinfo[:, 0:1]).astype(jnp.bfloat16)
    picked = jnp.dot(hot, pw[...], preferred_element_type=F32).astype(jnp.bfloat16)
    for i in range(NX):
        hs[i] = picked[:, LANES * i:LANES * (i + 1)]
    h_x = [send(hs.at[xs[d]], hxr.at[d - 1], x_peer[d]) for d in range(1, NX)]

    loaded(reward)
    rp[pl.ds(other, HALF), :v] = nt_dot(rh[pl.ds(other, HALF), :], rw[...])
    core_r = send(rp.at[pl.ds(other, HALF), :], rr, core_peer)
    rp[pl.ds(own, HALF), :v] = nt_dot(rh[pl.ds(own, HALF), :], rw[...])
    def r1():
        landed([core_r])
        stats = []
        for c in range(NCH):
            rows = pl.ds(pl.multiple_of(own + RC * c, RC), RC)
            logit = rp[rows, :] + rr[pl.ds(RC * c, RC), :]
            logit = jnp.where(lane < v, logit, LOW)
            m = jnp.max(logit, axis=1, keepdims=True)
            s = jnp.sum(jnp.exp(logit - m), axis=1, keepdims=True)
            is_target = (lane + first == colinfo[rows, 0:1]) & (lane < v)
            pick = jnp.sum(jnp.where(is_target, logit, 0.0), axis=1, keepdims=True)
            stats.append(jnp.where(st_lane == 0, m, jnp.where(st_lane == 1, s, jnp.where(st_lane == 2, pick, 0.0))))
        stats.append(jnp.zeros((256 - HALF, LANES), F32))
        rz[z] = jnp.transpose(jnp.concatenate(stats, axis=0))[:8, :]
        return [send(rz.at[z], rz.at[z], z_peer[d]) for d in range(1, NZ)]

    def merge_rows(buf, lo, hi):
        tiles = [buf[i] for i in range(lo, hi)]
        m = tiles[0][0:1]
        for t in tiles[1:]:
            m = jnp.maximum(m, t[0:1])
        s = jnp.zeros_like(m)
        pick = jnp.zeros_like(m)
        for t in tiles:
            s = s + jnp.exp(t[0:1] - m) * t[1:2]
            pick = pick + t[2:3]
        return m, s, pick

    def pack_rows(m, s, pick):
        row = lax.broadcasted_iota(jnp.int32, (8, 256), 0)
        return jnp.where(row == 0, m, jnp.where(row == 1, s, jnp.where(row == 2, pick, 0.0)))

    def h2():
        landed(h_x)
        h_own = hs[x].astype(F32)
        for d in range(1, NX):
            h_own = h_own + hxr[d - 1].astype(F32)
        hz[...] = h_own.reshape(2, NCH, RC, LANES)
        return [send(z_part(hz, zs_[d]), hzr.at[d - 1], z_peer[d]) for d in range(1, NZ)]

    per_blk = RC // ZR

    def z_part(ref, zz):
        return ref.at[lax.div(zz, per_blk), :, pl.ds(pl.multiple_of(lax.rem(zz, per_blk) * ZR, ZR), ZR), :]

    def r2(r_z):
        landed(r_z)
        rx[x] = pack_rows(*merge_rows(rz, 0, NZ))
        return [send(rx.at[x], rx.at[x], x_peer[d]) for d in range(1, NX)]

    def r3(r_x):
        landed(r_x)
        ry[y] = pack_rows(*merge_rows(rx, 0, NX))
        return [send(ry.at[y], ry.at[y], y_peer[d]) for d in range(1, NY)]

    def r4(r_y):
        landed(r_y)
        logp = []
        for s_ in range(2):
            m, s, pick = merge_rows(ry, s_ * NYL, (s_ + 1) * NYL)
            logp.append(pick - m - jnp.log(s))
        live = rowinfo[0:1, pl.ds(pl.multiple_of(tok * 256, 256), 256)].astype(F32)
        rc[tok] = jnp.broadcast_to(BETA * live * (logp[0] - logp[1]), (8, 256))
        return [send(rc.at[tok], rc.at[tok], core_peer)]

    def r5(r_c):
        landed(r_c)
        row = jnp.concatenate([rc[0], rc[1]], axis=1)
        rew[...] = jnp.concatenate([rc[0, 0:1, :HALF], rc[1, 0:1, :HALF]], axis=1).reshape(W)
        spot = lax.broadcasted_iota(jnp.int32, (RC, 512), 1)
        block = spot // 256
        inside = spot - 256 * block
        token = block * HALF + inside
        for t0 in range(0, W, RC):
            mine = t0 + lax.broadcasted_iota(jnp.int32, (RC, 512), 0)
            info = colinfo[t0:t0 + RC, :]
            same = (info[:, 2:3] == rowinfo[1:2, :]) & (token >= mine) & (inside < HALF)
            ret = jnp.sum(jnp.where(same, row[0:1], 0.0), axis=1, keepdims=True)
            wv[t0:t0 + RC, :] = jnp.broadcast_to(ret * info[:, 1:2].astype(F32), (RC, LANES))

    def h3(h_z):
        landed(h_z)
        total = z_part(hz, z)[...]
        for d in range(1, NZ):
            total = total + hzr[d - 1]
        hfin[...] = total

    live_copies = {}

    def stage_a(c):
        rows = pl.ds(pl.multiple_of(own + RC * c, RC), RC)
        q = qr[pl.ds(RC * c, RC), :].astype(jnp.int32).astype(F32)
        scale = jnp.exp(q[:, vp - 1:vp] * STEP) * (1.0 / FULL)
        logit = jnp.where(lane < v, pp[rows, :] + q * scale, LOW)
        m = jnp.max(logit, axis=1, keepdims=True)
        e = jnp.exp(logit - m)
        is_target = (lane + first == colinfo[rows, 0:1]) & (lane < v)
        e_rest = jnp.where(is_target, 0.0, e)
        s_rest = jnp.sum(e_rest, axis=1, keepdims=True)
        s_target = jnp.sum(jnp.where(is_target, e, 0.0), axis=1, keepdims=True)
        eb[rows, :] = e_rest.astype(eb.dtype)
        st[rows, :] = jnp.where(st_lane == 0, m, jnp.where(st_lane == 1, s_rest, s_target))
        live_copies["e", c] = [
            send(eb.at[rows, :], eb.at[rows, :], core_peer),
            send(st.at[rows, :], st.at[rows, :], core_peer),
        ]

    def split3(s, ref):
        ln = lax.broadcasted_iota(jnp.int32, s.shape, 1)
        left = jnp.where(ln < 3, s[:, 0:1], jnp.where(ln < 6, s[:, 1:2], s[:, 2:3]))
        part = lax.rem(ln, 3)
        for i in range(2):
            ref[...] = left.astype(ref.dtype)
            left = jnp.where(part > i, left - ref[...].astype(F32), left)
        ref[...] = left.astype(ref.dtype)

    def stage_b(c):
        landed(live_copies["e", c])
        r0, r1 = RC * c, HALF + RC * c
        e = jnp.concatenate([eb[r0:r0 + RC, :v], eb[r1:r1 + RC, :v]], axis=0)
        split3(jnp.concatenate([st[r0:r0 + RC, :], st[r1:r1 + RC, :]], axis=0), gs.at[c, 0, 1])
        s = gs[c, 0, 1]
        g = jnp.dot(e, pw[...], preferred_element_type=F32)
        for i in range(NX):
            gs[c, i, 0] = g[:, LANES * i:LANES * (i + 1)].astype(gs.dtype)
            if i:
                gs[c, i, 1] = s
        live_copies["x", c] = [send(gs.at[c, xs[d]], xr.at[c, d - 1], x_peer[d]) for d in range(1, NX)]

    def merge(gl, sl):
        m = sl[0][:, 0:1]
        for s in sl[1:]:
            m = jnp.maximum(m, s[:, 0:1])
        g_all = s_all = None
        for g, s in zip(gl, sl):
            a = jnp.exp(s[:, 0:1] - m)
            g_all = a * g if g_all is None else g_all + a * g
            s_all = a * s if s_all is None else s_all + a * s
        ln = lax.broadcasted_iota(jnp.int32, s_all.shape, 1)
        return g_all, jnp.where(ln == 0, m, s_all)

    def merge_parts(gl, tl):
        tl = [t.astype(F32) for t in tl]
        ml = [t[:, 0:1] + t[:, 1:2] + t[:, 2:3] for t in tl]
        m = ml[0]
        for other_m in ml[1:]:
            m = jnp.maximum(m, other_m)
        g_all = t_all = None
        for g, t, mi in zip(gl, tl, ml):
            a = jnp.exp(mi - m)
            g = a * g.astype(F32)
            t = a * t
            g_all = g if g_all is None else g_all + g
            t_all = t if t_all is None else t_all + t
        ln = lax.broadcasted_iota(jnp.int32, t_all.shape, 1)
        r, s = (t_all[:, i:i + 1] + t_all[:, i + 1:i + 2] + t_all[:, i + 2:i + 3] for i in (3, 6))
        return g_all, jnp.where(ln == 0, m, jnp.where(ln == 1, r, s))

    def stage_c(c):
        landed(live_copies["x", c])
        gl = [gs[c, x, 0]] + [xr[c, d, 0] for d in range(NX - 1)]
        tl = [gs[c, x, 1]] + [xr[c, d, 1] for d in range(NX - 1)]
        g, s = merge_parts(gl, tl)
        zs[c, 0] = g
        zs[c, 1] = s
        live_copies["z", c] = [
            send(zs.at[c, :, pl.ds(pl.multiple_of(zs_[d] * ZR, ZR), ZR), :], zr.at[c, d - 1], z_peer[d])
            for d in range(1, NZ)
        ]

    def stage_d(c):
        landed(live_copies["z", c])
        mine = pl.ds(pl.multiple_of(z * ZR, ZR), ZR)
        gl = [zs[c, 0, mine, :]] + [zr[c, d, 0] for d in range(NZ - 1)]
        sl = [zs[c, 1, mine, :]] + [zr[c, d, 1] for d in range(NZ - 1)]
        g, s = merge(gl, sl)
        yr[c, ylo, 0] = g
        yr[c, ylo, 1] = s
        yr[c, ylo, 2] = hfin[c]
        live_copies["y", c] = [send(yr.at[c, ylo], yr.at[c, ylo], yl_peer[d]) for d in range(1, NYL)]

    def stage_e(c):
        landed(live_copies["y", c])
        g, s = merge([yr[c, i, 0] for i in range(NYL)], [yr[c, i, 1] for i in range(NYL)])
        h = yr[c, 0, 2]
        for i in range(1, NYL):
            h = h + yr[c, i, 2]
        rest, target = s[:, 1:2], s[:, 2:3]
        scale = 1.0 / (rest + target)
        mine = pl.ds(pl.multiple_of(z * ZR, ZR), ZR)
        zag[c, mine, :] = scale * (g - rest * h)
        live_copies["zag", c] = [send(zag.at[c, mine, :], zag.at[c, mine, :], z_peer[d]) for d in range(1, NZ)]

    def stage_f(c):
        landed(live_copies["zag", c])
        weight = jnp.concatenate([wv[RC * c:RC * (c + 1), :], wv[HALF + RC * c:HALF + RC * (c + 1), :]], axis=0)
        hx[c, x] = (weight * zag[c]).astype(hx.dtype)
        live_copies["xag", c] = [send(hx.at[c, x], hx.at[c, x], x_peer[d]) for d in range(1, NX)]

    def stage_g(c):
        landed(live_copies["xag", c])
        for i in range(NX):
            for b in range(2):
                hg[HALF * b + RC * c:HALF * b + RC * (c + 1), LANES * i:LANES * (i + 1)] = hx[c, i, RC * b:RC * (b + 1), :]

    chain = {
        "S": side_step, "A": stage_a, "B": stage_b, "C": stage_c, "D": stage_d, "E": stage_e, "F": stage_f, "G": stage_g,
    }
    order = (
        "S0", "r1", "S1", "A0", "B0", "S2", "h2", "S3", "A1", "B1", "C0", "r2", "S4", "S5", "A2",
        "B2", "C1", "h3", "D0", "r3", "S6", "S7", "A3", "B3", "C2", "D1", "S8", "S9", "A4", "B4",
        "C3", "D2", "E0", "E1", "C4", "r4", "E2", "D3", "r5", "F0", "D4", "E3", "F1", "G0", "E4",
        "F2", "G1", "F3", "G2", "F4", "G3", "G4",
    )
    for word in order:
        if word == "h2":
            h_z = h2()
        elif word == "h3":
            h3(h_z)
        elif word == "r1":
            r_z = r1()
        elif word == "r2":
            r_x = r2(r_z)
        elif word == "r3":
            r_y = r3(r_x)
        elif word == "r4":
            r_c = r4(r_y)
        elif word == "r5":
            r5(r_c)
        else:
            chain[word[0]](int(word[1:]))
    for c in copies:
        if all(c is not w for w in waited):
            c.wait_send()


def hand_over(rew, hg, rew_out, hg_out):
    rew_out[...] = rew[...]
    hg_out[...] = hg[...]


def per_device(rh, rw, ph, pw, targets, mask, ids):
    v = rw.shape[2]
    rw, pw = jnp.swapaxes(rw, 1, 2), jnp.swapaxes(pw, 0, 1)
    feats, depth = ph.shape[1], rh.shape[2]
    vp = -(-v // LANES) * LANES
    if vp == v:
        vp += LANES
    bf, i16 = jnp.bfloat16, jnp.int16
    vm = pltpu.VMEM
    scratch = [
        vm((W, depth), bf), vm((v, depth), bf), vm((W, feats), bf), vm((v, feats), bf),
        vm((W, vp), F32), vm((HALF, vp), F32), vm((HALF, vp), i16), vm((HALF, vp), i16),
        vm((W, vp), bf), vm((W, LANES), F32),
        vm((W, vp), F32), vm((HALF, vp), F32),
        vm((NCH, NX, 2, CR, LANES), bf), vm((NCH, NX - 1, 2, CR, LANES), bf),
        vm((NCH, 2, CR, LANES), F32), vm((NCH, NZ - 1, 2, ZR, LANES), F32),
        vm((NCH, NYL, 3, ZR, LANES), F32), vm((NCH, CR, LANES), F32), vm((NCH, NX, CR, LANES), bf),
        vm((NX, W, LANES), bf), vm((NX - 1, W, LANES), bf), vm((2, NCH, RC, LANES), F32),
        vm((NZ - 1, NCH, ZR, LANES), F32), vm((NCH, ZR, LANES), F32),
        vm((NZ, 8, 256), F32), vm((NX, 8, 256), F32), vm((NY, 8, 256), F32), vm((2, 8, 256), F32),
        vm((W, LANES), F32), vm((W, LANES), jnp.int32), vm((8, 512), jnp.int32),
        vm((W,), jnp.int32), vm((W,), jnp.int32), vm((W,), jnp.int32),
        pltpu.SemaphoreType.DMA((16,)), pltpu.SemaphoreType.DMA((NSEM,)), pltpu.SemaphoreType.DMA((NSEM,)),
    ]
    vspec = pl.BlockSpec(memory_space=pltpu.VMEM)
    hspec = pl.BlockSpec(memory_space=pltpu.HBM)
    rew, hg = pl.pallas_call(
        functools.partial(kernel, v),
        out_shape=(jax.ShapeDtypeStruct((W,), F32), jax.ShapeDtypeStruct((W, feats), bf)),
        in_specs=[hspec] * 7,
        out_specs=(vspec, vspec),
        scratch_shapes=scratch,
        compiler_params=pltpu.CompilerParams(
            collective_id=0, has_side_effects=True, vmem_limit_bytes=60 << 20
        ),
    )(rh, rw, ph, pw, targets, mask, ids)
    return pl.pallas_call(
        hand_over,
        out_shape=(jax.ShapeDtypeStruct((W,), F32), jax.ShapeDtypeStruct((W, feats), bf)),
        in_specs=[vspec, vspec],
        out_specs=(vspec, vspec),
    )(rew, hg)


def solution(mesh):
    placed = (
        P("side", None, "tok"),
        P("side", "tok", "vocab"),
        P(None, ("side", "tok")),
        P(("side", "tok"), "vocab"),
        P(),
        P(),
        P(),
    )
    return jax.shard_map(
        per_device,
        mesh=mesh,
        in_specs=placed,
        out_specs=(P(), P(None, ("side", "tok"))),
        check_vma=False,
    )
```

```python
import functools
import math

import jax
import jax.numpy as jnp
from jax import lax
from jax.experimental import pallas as pl
from jax.experimental.pallas import tpu as pltpu
from jax.sharding import PartitionSpec as P

BETA = 0.05
MESH = pl.DeviceIdType.MESH
F32 = jnp.float32
NX, NYL, NZ = 4, 4, 8
NY = 2 * NYL
W = 320
HALF = 160
RC = 32
NCH = HALF // RC
SR = 16
WINDOW = 4
CR = 2 * RC
ZR = CR // NZ
LANES = 128
STEP = math.log(2.0) / 16.0
FULL = 32700.0
LOW = -1e30
NSEM = 256


def nt_dot(a, b):
    return lax.dot_general(a, b, (((1,), (1,)), ((), ())), preferred_element_type=F32)


def kernel(
    v,
    rh_hbm, rw_hbm, ph_hbm, pw_hbm, t_hbm, m_hbm, i_hbm,
    rew, hg,
    rh, rw, ph, pw, pp, pr, qs, qr, eb, st,
    rp, rr, gs, xr, zs, zr, yr, zag, hx,
    hs, hxr, hz, hzr, hfin, rz, rx, ry, rc, wv, colinfo, rowinfo, targets, mask, ids,
    load_sem, send_sem, recv_sem,
):
    vp = pp.shape[1]
    feats = ph.shape[1]
    side = lax.axis_index("side")
    vocab = lax.axis_index("vocab")
    tok = lax.axis_index("tok")
    ylo = lax.div(vocab, NX * NZ)
    x = lax.rem(lax.div(vocab, NZ), NX)
    z = lax.rem(vocab, NZ)
    y = side * NYL + ylo
    first = vocab * v

    def at(yy, xx, zz, tt):
        return (lax.div(yy, NYL), lax.rem(yy, NYL) * (NX * NZ) + xx * NZ + zz, tt)

    core_peer = at(y, x, z, 1 - tok)
    side_peer = at(lax.rem(y + NYL, NY), x, z, tok)
    xs = [lax.rem(x + d, NX) for d in range(NX)]
    zs_ = [lax.rem(z + d, NZ) for d in range(NZ)]
    x_peer = [at(y, xs[d], z, tok) for d in range(NX)]
    z_peer = [at(y, x, zs_[d], tok) for d in range(NZ)]
    y_peer = [at(lax.rem(y + d, NY), x, z, tok) for d in range(NY)]
    yls = [lax.rem(ylo + d, NYL) for d in range(NYL)]
    yl_peer = [at(side * NYL + yls[d], x, z, tok) for d in range(NYL)]

    loads = []

    def load(src, dst, pieces=1):
        step = -(-src.shape[0] // (16 * pieces)) * 16
        group = []
        for r in range(0, src.shape[0], step):
            part = pl.ds(r, min(step, src.shape[0] - r))
            group.append(pltpu.make_async_copy(src.at[part], dst.at[part], load_sem.at[len(loads)]))
            loads.append(group[-1])
            group[-1].start()
        return group

    def loaded(group):
        for c in group:
            c.wait()

    policy = load(pw_hbm, pw, 4) + load(ph_hbm, ph)
    lists_in = [load(t_hbm, targets), load(m_hbm, mask), load(i_hbm, ids)]

    barrier = pltpu.get_barrier_semaphore()
    peers = [core_peer] + x_peer[1:] + z_peer[1:] + y_peer[1:]
    for p in peers:
        pl.semaphore_signal(barrier, inc=1, device_id=p, device_id_type=MESH)

    copies = []

    def send(src, dst, peer):
        i = len(copies)
        c = pltpu.make_async_remote_copy(
            src_ref=src, dst_ref=dst, send_sem=send_sem.at[i], recv_sem=recv_sem.at[i],
            device_id=peer, device_id_type=MESH,
        )
        c.start()
        copies.append(c)
        return c

    def landed(group):
        for c in group:
            c.wait_recv()

    for c in lists_in:
        loaded(c)
    lists = [r[...].reshape(1, W) for r in (targets, mask, ids)]
    rows3 = jnp.concatenate(lists + [jnp.zeros((5, W), jnp.int32)], axis=0).astype(F32)
    rows3 = jnp.concatenate([rows3, jnp.zeros((LANES - 8, W), F32)], axis=0)
    rows3 = jnp.concatenate([rows3, jnp.zeros((LANES, 384 - W), F32)], axis=1)
    colinfo[...] = jnp.transpose(rows3)[:W].astype(jnp.int32)
    for b in range(2):
        half = jnp.concatenate([r[:, HALF * b:HALF * (b + 1)] for r in lists[1:]], axis=0)
        rowinfo[0:2, 256 * b:256 * b + HALF] = half
        rowinfo[0:2, 256 * b + HALF:256 * (b + 1)] = jnp.zeros((2, 256 - HALF), jnp.int32)

    tail = vp - LANES
    for buf in (pp, rp):
        buf[:, tail:] = jnp.zeros((W, LANES), F32)
    eb[:, tail:] = jnp.zeros((W, LANES), eb.dtype)

    own = pl.multiple_of(tok * HALF, HALF)
    other = pl.multiple_of((1 - tok) * HALF, HALF)

    loaded(policy)
    reward = load(rh_hbm.at[0], rh) + load(rw_hbm.at[0], rw, 4)
    pp[pl.ds(other, HALF), :v] = nt_dot(ph[pl.ds(other, HALF), :], pw[...])
    pl.semaphore_wait(barrier, len(peers))
    core_p = []
    for c in range(NCH):
        core_p.append(send(pp.at[pl.ds(other + RC * c, RC), :], pr.at[pl.ds(RC * c, RC), :], core_peer))
    pp[pl.ds(own, HALF), :v] = nt_dot(ph[pl.ds(own, HALF), :], pw[...])

    lane = lax.broadcasted_iota(jnp.int32, (RC, vp), 1)
    st_lane = lax.broadcasted_iota(jnp.int32, (RC, LANES), 1)

    side_p = []

    def side_send():
        rows = pl.ds(SR * len(side_p), SR)
        side_p.append(send(qs.at[rows, :], qr.at[rows, :], side_peer))

    def side_step(i):
        landed([side_p[i]])
        if len(side_p) < HALF // SR:
            side_p[i].wait_send()
            waited.append(side_p[i])
            side_send()

    waited = []
    for c in range(NCH):
        landed([core_p[c]])
        rows = pl.ds(pl.multiple_of(own + RC * c, RC), RC)
        part = pp[rows, :] + pr[pl.ds(RC * c, RC), :]
        pp[rows, :] = part
        top = jnp.maximum(jnp.max(jnp.abs(part), axis=1, keepdims=True), 1e-6)
        expo = jnp.ceil(jnp.log(top) / STEP)
        inv = FULL * jnp.exp(expo * -STEP)
        quant = jnp.clip(jnp.round(part * inv), -32767.0, 32767.0)
        quant = jnp.where(lane == vp - 1, expo, quant)
        qs[pl.ds(RC * c, RC), :] = quant.astype(jnp.int32).astype(jnp.int16)
        for _ in range(2):
            if len(side_p) < WINDOW:
                side_send()

    wide = lax.broadcasted_iota(jnp.int32, (W, v), 1) + first
    hot = (wide == colinfo[:, 0:1]).astype(jnp.bfloat16)
    picked = jnp.dot(hot, pw[...], preferred_element_type=F32).astype(jnp.bfloat16)
    for i in range(NX):
        hs[i] = picked[:, LANES * i:LANES * (i + 1)]
    h_x = [send(hs.at[xs[d]], hxr.at[d - 1], x_peer[d]) for d in range(1, NX)]

    loaded(reward)
    rp[pl.ds(other, HALF), :v] = nt_dot(rh[pl.ds(other, HALF), :], rw[...])
    core_r = send(rp.at[pl.ds(other, HALF), :], rr, core_peer)
    rp[pl.ds(own, HALF), :v] = nt_dot(rh[pl.ds(own, HALF), :], rw[...])
    def r1():
        landed([core_r])
        stats = []
        for c in range(NCH):
            rows = pl.ds(pl.multiple_of(own + RC * c, RC), RC)
            logit = rp[rows, :] + rr[pl.ds(RC * c, RC), :]
            logit = jnp.where(lane < v, logit, LOW)
            m = jnp.max(logit, axis=1, keepdims=True)
            s = jnp.sum(jnp.exp(logit - m), axis=1, keepdims=True)
            is_target = (lane + first == colinfo[rows, 0:1]) & (lane < v)
            pick = jnp.sum(jnp.where(is_target, logit, 0.0), axis=1, keepdims=True)
            stats.append(jnp.where(st_lane == 0, m, jnp.where(st_lane == 1, s, jnp.where(st_lane == 2, pick, 0.0))))
        stats.append(jnp.zeros((256 - HALF, LANES), F32))
        rz[z] = jnp.transpose(jnp.concatenate(stats, axis=0))[:8, :]
        return [send(rz.at[z, pl.ds(0, 4), :], rz.at[z, pl.ds(0, 4), :], z_peer[d]) for d in range(1, NZ)]

    def merge_rows(buf, lo, hi):
        tiles = [buf[i] for i in range(lo, hi)]
        m = tiles[0][0:1]
        for t in tiles[1:]:
            m = jnp.maximum(m, t[0:1])
        s = jnp.zeros_like(m)
        pick = jnp.zeros_like(m)
        for t in tiles:
            s = s + jnp.exp(t[0:1] - m) * t[1:2]
            pick = pick + t[2:3]
        return m, s, pick

    def pack_rows(m, s, pick):
        row = lax.broadcasted_iota(jnp.int32, (8, 256), 0)
        return jnp.where(row == 0, m, jnp.where(row == 1, s, jnp.where(row == 2, pick, 0.0)))

    def h2():
        landed(h_x)
        h_own = hs[x].astype(F32)
        for d in range(1, NX):
            h_own = h_own + hxr[d - 1].astype(F32)
        hz[...] = h_own.reshape(2, NCH, RC, LANES)
        return [send(z_part(hz, zs_[d]), hzr.at[d - 1], z_peer[d]) for d in range(1, NZ)]

    per_blk = RC // ZR

    def z_part(ref, zz):
        return ref.at[lax.div(zz, per_blk), :, pl.ds(pl.multiple_of(lax.rem(zz, per_blk) * ZR, ZR), ZR), :]

    def r2(r_z):
        landed(r_z)
        rx[x] = pack_rows(*merge_rows(rz, 0, NZ))
        return [send(rx.at[x, pl.ds(0, 4), :], rx.at[x, pl.ds(0, 4), :], x_peer[d]) for d in range(1, NX)]

    def r3(r_x):
        landed(r_x)
        ry[y] = pack_rows(*merge_rows(rx, 0, NX))
        return [send(ry.at[y, pl.ds(0, 4), :], ry.at[y, pl.ds(0, 4), :], y_peer[d]) for d in range(1, NY)]

    def r4(r_y):
        landed(r_y)
        logp = []
        for s_ in range(2):
            m, s, pick = merge_rows(ry, s_ * NYL, (s_ + 1) * NYL)
            logp.append(pick - m - jnp.log(s))
        live = rowinfo[0:1, pl.ds(pl.multiple_of(tok * 256, 256), 256)].astype(F32)
        rc[tok] = jnp.broadcast_to(BETA * live * (logp[0] - logp[1]), (8, 256))
        return [send(rc.at[tok], rc.at[tok], core_peer)]

    def r5(r_c):
        landed(r_c)
        row = jnp.concatenate([rc[0], rc[1]], axis=1)
        rew[...] = jnp.concatenate([rc[0, 0:1, :HALF], rc[1, 0:1, :HALF]], axis=1).reshape(W)
        spot = lax.broadcasted_iota(jnp.int32, (RC, 512), 1)
        block = spot // 256
        inside = spot - 256 * block
        token = block * HALF + inside
        for t0 in range(0, W, RC):
            mine = t0 + lax.broadcasted_iota(jnp.int32, (RC, 512), 0)
            info = colinfo[t0:t0 + RC, :]
            same = (info[:, 2:3] == rowinfo[1:2, :]) & (token >= mine) & (inside < HALF)
            ret = jnp.sum(jnp.where(same, row[0:1], 0.0), axis=1, keepdims=True)
            wv[t0:t0 + RC, :] = jnp.broadcast_to(ret * info[:, 1:2].astype(F32), (RC, LANES))

    def h3(h_z):
        landed(h_z)
        total = z_part(hz, z)[...]
        for d in range(1, NZ):
            total = total + hzr[d - 1]
        hfin[...] = total

    live_copies = {}

    def stage_a(c):
        rows = pl.ds(pl.multiple_of(own + RC * c, RC), RC)
        q = qr[pl.ds(RC * c, RC), :].astype(jnp.int32).astype(F32)
        scale = jnp.exp(q[:, vp - 1:vp] * STEP) * (1.0 / FULL)
        logit = jnp.where(lane < v, pp[rows, :] + q * scale, LOW)
        m = jnp.max(logit, axis=1, keepdims=True)
        e = jnp.exp(logit - m)
        is_target = (lane + first == colinfo[rows, 0:1]) & (lane < v)
        e_rest = jnp.where(is_target, 0.0, e)
        s_rest = jnp.sum(e_rest, axis=1, keepdims=True)
        s_target = jnp.sum(jnp.where(is_target, e, 0.0), axis=1, keepdims=True)
        eb[rows, :] = e_rest.astype(eb.dtype)
        st[rows, :] = jnp.where(st_lane == 0, m, jnp.where(st_lane == 1, s_rest, s_target))
        live_copies["e", c] = [
            send(eb.at[rows, :], eb.at[rows, :], core_peer),
            send(st.at[rows, :], st.at[rows, :], core_peer),
        ]

    def split3(s, ref):
        ln = lax.broadcasted_iota(jnp.int32, s.shape, 1)
        left = jnp.where(ln < 3, s[:, 0:1], jnp.where(ln < 6, s[:, 1:2], s[:, 2:3]))
        part = lax.rem(ln, 3)
        for i in range(2):
            ref[...] = left.astype(ref.dtype)
            left = jnp.where(part > i, left - ref[...].astype(F32), left)
        ref[...] = left.astype(ref.dtype)

    def stage_b(c):
        landed(live_copies["e", c])
        r0, r1 = RC * c, HALF + RC * c
        e = jnp.concatenate([eb[r0:r0 + RC, :v], eb[r1:r1 + RC, :v]], axis=0)
        split3(jnp.concatenate([st[r0:r0 + RC, :], st[r1:r1 + RC, :]], axis=0), gs.at[c, 0, 1])
        s = gs[c, 0, 1]
        g = jnp.dot(e, pw[...], preferred_element_type=F32)
        for i in range(NX):
            gs[c, i, 0] = g[:, LANES * i:LANES * (i + 1)].astype(gs.dtype)
            if i:
                gs[c, i, 1] = s
        live_copies["x", c] = [send(gs.at[c, xs[d]], xr.at[c, d - 1], x_peer[d]) for d in range(1, NX)]

    def merge(gl, sl):
        m = sl[0][:, 0:1]
        for s in sl[1:]:
            m = jnp.maximum(m, s[:, 0:1])
        g_all = s_all = None
        for g, s in zip(gl, sl):
            a = jnp.exp(s[:, 0:1] - m)
            g_all = a * g if g_all is None else g_all + a * g
            s_all = a * s if s_all is None else s_all + a * s
        ln = lax.broadcasted_iota(jnp.int32, s_all.shape, 1)
        return g_all, jnp.where(ln == 0, m, s_all)

    def merge_parts(gl, tl):
        tl = [t.astype(F32) for t in tl]
        ml = [t[:, 0:1] + t[:, 1:2] + t[:, 2:3] for t in tl]
        m = ml[0]
        for other_m in ml[1:]:
            m = jnp.maximum(m, other_m)
        g_all = t_all = None
        for g, t, mi in zip(gl, tl, ml):
            a = jnp.exp(mi - m)
            g = a * g.astype(F32)
            t = a * t
            g_all = g if g_all is None else g_all + g
            t_all = t if t_all is None else t_all + t
        ln = lax.broadcasted_iota(jnp.int32, t_all.shape, 1)
        r, s = (t_all[:, i:i + 1] + t_all[:, i + 1:i + 2] + t_all[:, i + 2:i + 3] for i in (3, 6))
        return g_all, jnp.where(ln == 0, m, jnp.where(ln == 1, r, s))

    def stage_c(c):
        landed(live_copies["x", c])
        gl = [gs[c, x, 0]] + [xr[c, d, 0] for d in range(NX - 1)]
        tl = [gs[c, x, 1]] + [xr[c, d, 1] for d in range(NX - 1)]
        g, s = merge_parts(gl, tl)
        zs[c, 0] = g
        zs[c, 1] = s
        live_copies["z", c] = [
            send(zs.at[c, :, pl.ds(pl.multiple_of(zs_[d] * ZR, ZR), ZR), :], zr.at[c, d - 1], z_peer[d])
            for d in range(1, NZ)
        ]

    def stage_d(c):
        landed(live_copies["z", c])
        mine = pl.ds(pl.multiple_of(z * ZR, ZR), ZR)
        gl = [zs[c, 0, mine, :]] + [zr[c, d, 0] for d in range(NZ - 1)]
        sl = [zs[c, 1, mine, :]] + [zr[c, d, 1] for d in range(NZ - 1)]
        g, s = merge(gl, sl)
        yr[c, ylo, 0] = g
        yr[c, ylo, 1] = s
        yr[c, ylo, 2] = hfin[c]
        live_copies["y", c] = [send(yr.at[c, ylo], yr.at[c, ylo], yl_peer[d]) for d in range(1, NYL)]

    def stage_e(c):
        landed(live_copies["y", c])
        g, s = merge([yr[c, i, 0] for i in range(NYL)], [yr[c, i, 1] for i in range(NYL)])
        h = yr[c, 0, 2]
        for i in range(1, NYL):
            h = h + yr[c, i, 2]
        rest, target = s[:, 1:2], s[:, 2:3]
        scale = 1.0 / (rest + target)
        mine = pl.ds(pl.multiple_of(z * ZR, ZR), ZR)
        zag[c, mine, :] = scale * (g - rest * h)
        live_copies["zag", c] = [send(zag.at[c, mine, :], zag.at[c, mine, :], z_peer[d]) for d in range(1, NZ)]

    def stage_f(c):
        landed(live_copies["zag", c])
        weight = jnp.concatenate([wv[RC * c:RC * (c + 1), :], wv[HALF + RC * c:HALF + RC * (c + 1), :]], axis=0)
        hx[c, x] = (weight * zag[c]).astype(hx.dtype)
        live_copies["xag", c] = [send(hx.at[c, x], hx.at[c, x], x_peer[d]) for d in range(1, NX)]

    def stage_g(c):
        landed(live_copies["xag", c])
        for i in range(NX):
            for b in range(2):
                hg[HALF * b + RC * c:HALF * b + RC * (c + 1), LANES * i:LANES * (i + 1)] = hx[c, i, RC * b:RC * (b + 1), :]

    chain = {
        "S": side_step, "A": stage_a, "B": stage_b, "C": stage_c, "D": stage_d, "E": stage_e, "F": stage_f, "G": stage_g,
    }
    order = (
        "S0", "r1", "S1", "A0", "B0", "S2", "h2", "S3", "A1", "B1", "C0", "r2", "S4", "S5", "A2",
        "B2", "C1", "h3", "D0", "r3", "S6", "S7", "A3", "B3", "C2", "D1", "S8", "S9", "A4", "B4",
        "C3", "D2", "E0", "E1", "C4", "r4", "E2", "D3", "r5", "F0", "D4", "E3", "F1", "G0", "E4",
        "F2", "G1", "F3", "G2", "F4", "G3", "G4",
    )
    for word in order:
        if word == "h2":
            h_z = h2()
        elif word == "h3":
            h3(h_z)
        elif word == "r1":
            r_z = r1()
        elif word == "r2":
            r_x = r2(r_z)
        elif word == "r3":
            r_y = r3(r_x)
        elif word == "r4":
            r_c = r4(r_y)
        elif word == "r5":
            r5(r_c)
        else:
            chain[word[0]](int(word[1:]))
    for c in copies:
        if all(c is not w for w in waited):
            c.wait_send()


def hand_over(rew, hg, rew_out, hg_out):
    rew_out[...] = rew[...]
    hg_out[...] = hg[...]


def per_device(rh, rw, ph, pw, targets, mask, ids):
    v = rw.shape[2]
    rw, pw = jnp.swapaxes(rw, 1, 2), jnp.swapaxes(pw, 0, 1)
    feats, depth = ph.shape[1], rh.shape[2]
    vp = -(-v // LANES) * LANES
    if vp == v:
        vp += LANES
    bf, i16 = jnp.bfloat16, jnp.int16
    vm = pltpu.VMEM
    scratch = [
        vm((W, depth), bf), vm((v, depth), bf), vm((W, feats), bf), vm((v, feats), bf),
        vm((W, vp), F32), vm((HALF, vp), F32), vm((HALF, vp), i16), vm((HALF, vp), i16),
        vm((W, vp), bf), vm((W, LANES), F32),
        vm((W, vp), F32), vm((HALF, vp), F32),
        vm((NCH, NX, 2, CR, LANES), bf), vm((NCH, NX - 1, 2, CR, LANES), bf),
        vm((NCH, 2, CR, LANES), F32), vm((NCH, NZ - 1, 2, ZR, LANES), F32),
        vm((NCH, NYL, 3, ZR, LANES), F32), vm((NCH, CR, LANES), F32), vm((NCH, NX, CR, LANES), bf),
        vm((NX, W, LANES), bf), vm((NX - 1, W, LANES), bf), vm((2, NCH, RC, LANES), F32),
        vm((NZ - 1, NCH, ZR, LANES), F32), vm((NCH, ZR, LANES), F32),
        vm((NZ, 8, 256), F32), vm((NX, 8, 256), F32), vm((NY, 8, 256), F32), vm((2, 8, 256), F32),
        vm((W, LANES), F32), vm((W, LANES), jnp.int32), vm((8, 512), jnp.int32),
        vm((W,), jnp.int32), vm((W,), jnp.int32), vm((W,), jnp.int32),
        pltpu.SemaphoreType.DMA((16,)), pltpu.SemaphoreType.DMA((NSEM,)), pltpu.SemaphoreType.DMA((NSEM,)),
    ]
    vspec = pl.BlockSpec(memory_space=pltpu.VMEM)
    hspec = pl.BlockSpec(memory_space=pltpu.HBM)
    rew, hg = pl.pallas_call(
        functools.partial(kernel, v),
        out_shape=(jax.ShapeDtypeStruct((W,), F32), jax.ShapeDtypeStruct((W, feats), bf)),
        in_specs=[hspec] * 7,
        out_specs=(vspec, vspec),
        scratch_shapes=scratch,
        compiler_params=pltpu.CompilerParams(
            collective_id=0, has_side_effects=True, vmem_limit_bytes=60 << 20
        ),
    )(rh, rw, ph, pw, targets, mask, ids)
    return pl.pallas_call(
        hand_over,
        out_shape=(jax.ShapeDtypeStruct((W,), F32), jax.ShapeDtypeStruct((W, feats), bf)),
        in_specs=[vspec, vspec],
        out_specs=(vspec, vspec),
    )(rew, hg)


def solution(mesh):
    placed = (
        P("side", None, "tok"),
        P("side", "tok", "vocab"),
        P(None, ("side", "tok")),
        P(("side", "tok"), "vocab"),
        P(),
        P(),
        P(),
    )
    return jax.shard_map(
        per_device,
        mesh=mesh,
        in_specs=placed,
        out_specs=(P(), P(None, ("side", "tok"))),
        check_vma=False,
    )
```
